512 devices in a mesh: resp: 16 (over x, y_lo, core), ctx: 32 (over z, y_hi).
Axes of the slice: x: 4, y: 4 (y_hi: 2, y_lo: 2; y = y_hi * 2 + y_lo), z: 16, core: 2. Of those that a mesh axis runs over, the one named last changes fastest.
Arguments:
- queries: bfloat16 [16, 8192, 4096], P('resp', 'ctx'), may hold values from -6 to 6
- resp_kv: bfloat16 [16, 8192, 2, 512], P('resp', 'ctx'), may hold values from -6 to 6
- prompt_kv: bfloat16 [32, 128, 2, 512], P('ctx', 'resp'), may hold values from -6 to 6
- lengths: int32 [16], P('resp'), may hold values from 2048 to 8192, as said below
- block_slot: int32 [32], replicated, may hold values from 0 to 31, each once
Outputs:
- attended: bfloat16 [16, 8192, 4096], P('resp', 'ctx')
- log_total: float32 [16, 32, 8192], P('resp', None, 'ctx')
The draws below stay inside these ranges and needn't reach their ends.
Inputs may be any that keep to these rules, and one draw needn't show every extreme that they name: `lengths`: every response has at least 2048 live positions, and some response is live over all 8192.
All inputs are finite; a program needn't handle non-finite values.
Results may differ from the reference program's by a relative error of at most 0.007.
Values may be sent and summed in bfloat16 or wider, within the bound.
A program may use at most 64 MiB of HBM per device.

```python
import math
import jax
import jax.numpy as jnp
from jax import lax

QUERY_HEADS = 32
KEY_VALUE_HEADS = 4
HEAD_SIZE = 128
RESPONSE_BLOCK = 256
PROMPT_BLOCK = 128
RESPONSE_COUNT = 16
PROMPT_BLOCKS = 32
RESPONSE_LENGTH = 8192
N_CTX = 32


def draw_queries(key, part):
    key = jax.random.fold_in(key, 11)
    tensor_shape = (RESPONSE_COUNT, RESPONSE_LENGTH, QUERY_HEADS * HEAD_SIZE)
    base = jax.random.truncated_normal(key, -6.0, 6.0, tensor_shape, jnp.float32)
    return base.astype(jnp.bfloat16)


def draw_resp_kv(key, part):
    key = jax.random.fold_in(key, 23)
    tensor_shape = (RESPONSE_COUNT, RESPONSE_LENGTH, 2, KEY_VALUE_HEADS * HEAD_SIZE)
    base = jax.random.truncated_normal(key, -6.0, 6.0, tensor_shape, jnp.float32)
    return base.astype(jnp.bfloat16)


def draw_prompt_kv(key, part):
    key = jax.random.fold_in(key, 37)
    tensor_shape = (PROMPT_BLOCKS, PROMPT_BLOCK, 2, KEY_VALUE_HEADS * HEAD_SIZE)
    base = jax.random.truncated_normal(key, -6.0, 6.0, tensor_shape, jnp.float32)
    return base.astype(jnp.bfloat16)


def draw_lengths(key, part):
    key = jax.random.fold_in(key, 51)
    first_key, second_key = jax.random.split(key)
    picked = jax.random.randint(first_key, (RESPONSE_COUNT,), RESPONSE_LENGTH // 4, RESPONSE_LENGTH + 1)
    longest = jax.random.randint(second_key, (), 0, RESPONSE_COUNT)
    return jnp.where(jnp.arange(RESPONSE_COUNT) == longest, RESPONSE_LENGTH, picked).astype(jnp.int32)


def setup_inputs(seed: int = 0) -> dict:
    splits = jax.random.split(jax.random.key(seed), 6)
    return {
        "queries": draw_queries(jax.random.fold_in(splits[5], 71), 0),
        "resp_kv": draw_resp_kv(jax.random.fold_in(splits[5], 71), 0),
        "prompt_kv": draw_prompt_kv(jax.random.fold_in(splits[5], 71), 0),
        "lengths": draw_lengths(jax.random.fold_in(splits[5], 71), 0),
        "block_slot": jax.random.permutation(splits[4], N_CTX).astype(jnp.int32),
    }


NEGATIVE_FILL = -1e+30

def reference(queries, resp_kv, prompt_kv, lengths, block_slot):
    query_group_size = QUERY_HEADS // KEY_VALUE_HEADS
    scale = 1.0 / math.sqrt(HEAD_SIZE)
    offsets = jnp.arange(RESPONSE_BLOCK, dtype=jnp.int32)

    def per_response(item):
        query_all, kv_all, live_length = item

        def per_block(index):
            query_matrix = lax.dynamic_slice_in_dim(query_all, index * RESPONSE_BLOCK, RESPONSE_BLOCK, 0)
            query_matrix = query_matrix.astype(jnp.float32).reshape(RESPONSE_BLOCK, KEY_VALUE_HEADS, query_group_size, HEAD_SIZE)
            query_pos = block_slot[index].astype(jnp.int32) * RESPONSE_BLOCK + offsets
            prompt_rows = lax.dynamic_index_in_dim(prompt_kv, index, 0, keepdims=False)
            key_parts = [prompt_rows]
            mask_parts = [jnp.ones((RESPONSE_BLOCK, PROMPT_BLOCK), dtype=bool)]
            for back in range(3):
                source = ((index - back) % N_CTX).astype(jnp.int32)
                key_parts.append(lax.dynamic_slice_in_dim(kv_all, source * RESPONSE_BLOCK, RESPONSE_BLOCK, 0))
                key_pos = block_slot[source].astype(jnp.int32) * RESPONSE_BLOCK + offsets
                mask_parts.append((key_pos[None, :] <= query_pos[:, None]) & (key_pos[None, :] < live_length))
            both_sides = jnp.concatenate(key_parts, axis=0)
            key_ok = jnp.concatenate(mask_parts, axis=1)
            count_total = both_sides.shape[0]
            key_matrix = both_sides[:, 0].astype(jnp.float32).reshape(count_total, KEY_VALUE_HEADS, HEAD_SIZE)
            value_matrix = both_sides[:, 1].astype(jnp.float32).reshape(count_total, KEY_VALUE_HEADS, HEAD_SIZE)
            scores = jnp.einsum('qhgd,khd->hgqk', query_matrix, key_matrix) * scale
            scores = jnp.where(key_ok[None, None], scores, NEGATIVE_FILL)
            top = lax.optimization_barrier(jnp.max(scores, axis=-1))
            exps = jnp.exp(scores - top[..., None])
            total = lax.optimization_barrier(jnp.sum(exps, axis=-1))
            weights = exps.astype(jnp.bfloat16).astype(jnp.float32)
            summed = jnp.einsum('hgqk,khd->hgqd', weights, value_matrix)
            result = summed / total[..., None]
            result = jnp.transpose(result, (2, 0, 1, 3)).reshape(RESPONSE_BLOCK, QUERY_HEADS * HEAD_SIZE)
            is_live = query_pos < live_length
            result = jnp.where(is_live[:, None], result, 0.0).astype(jnp.bfloat16)
            log_part = (top + jnp.log(total)).reshape(QUERY_HEADS, RESPONSE_BLOCK)
            log_part = jnp.where(is_live[None, :], log_part, 0.0)
            return (result, log_part)
        results, logs = lax.map(per_block, jnp.arange(N_CTX, dtype=jnp.int32))
        return (results.reshape(RESPONSE_LENGTH, QUERY_HEADS * HEAD_SIZE), jnp.transpose(logs, (1, 0, 2)).reshape(QUERY_HEADS, RESPONSE_LENGTH))
    attended, log_total = lax.map(per_response, (queries, resp_kv, lengths))
    return (attended, log_total)
```

```python
import math

import jax
import jax.numpy as jnp
from jax import lax
from jax.experimental import pallas as pl
from jax.experimental.pallas import tpu as pltpu
from jax.sharding import PartitionSpec as P

QUERY_HEADS = 32
KEY_VALUE_HEADS = 4
GROUP = QUERY_HEADS // KEY_VALUE_HEADS
HEAD_SIZE = 128
ROWS = 256
PROMPT = 128
NEAR = ROWS + PROMPT
N_CTX = 32
N_RESP = 16
NEGATIVE_FILL = -1e30
LOG2_SCALE = math.log2(math.e) / math.sqrt(HEAD_SIZE)
LN2 = math.log(2.0)
F32 = jnp.float32
BF16 = jnp.bfloat16
NT = (((1,), (1,)), ((), ()))
MESH = pl.DeviceIdType.MESH


def at(resp, ctx):
    return {"resp": resp, "ctx": ctx}


def remote(src, dst, send_sem, recv_sem, target):
    return pltpu.make_async_remote_copy(
        src_ref=src,
        dst_ref=dst,
        send_sem=send_sem,
        recv_sem=recv_sem,
        device_id=target,
        device_id_type=MESH,
    )


def head_columns(head):
    return pl.ds(pl.multiple_of(head * HEAD_SIZE, HEAD_SIZE), HEAD_SIZE)


def kernel(
    q_hbm, kv_hbm, prompt_hbm, length_ref, slot_ref,
    out_ref, log_ref,
    q, kv_raw, prompt_raw, near_k, near_v, z_k, z_v, y_k, y_v,
    near_bias, near_top, near_sum, top_all, total_all,
    near_s, near_p, far_s, far_p,
    q_sem, kv_sem, own_sem, z_send, z_recv, y_send, y_recv,
    first_send, first_recv, second_send, second_recv, third_send, third_recv,
):
    r = lax.axis_index("resp")
    c = lax.axis_index("ctx")
    core = lax.rem(r, 2)
    pair = r // 2
    odd = lax.rem(c, 2)
    next_z = at(r, lax.rem(c + 2, N_CTX))
    prev_z = at(r, lax.rem(c + N_CTX - 2, N_CTX))
    across = at(r, c + 1 - 2 * odd)
    sibling = at(r + 1 - 2 * core, c)
    y_side = at(r + 2 - 4 * lax.rem(pair, 2), c)
    x_peers = [at(lax.rem(r + 4 * k, N_RESP), c) for k in (1, 2, 3)]

    barrier = pltpu.get_barrier_semaphore()
    for device in (prev_z, across, sibling, y_side, *x_peers):
        pl.semaphore_signal(barrier, inc=1, device_id=device, device_id_type=MESH)

    kv_copies = [
        pltpu.make_async_copy(
            kv_hbm.at[:, :, pl.ds(g * HEAD_SIZE, HEAD_SIZE)], kv_raw.at[g], kv_sem.at[g]
        )
        for g in range(KEY_VALUE_HEADS)
    ]
    for copy in kv_copies:
        copy.start()
    own_place = pl.ds((core * 8 + pair) * 8, 8)
    own_copy = pltpu.make_async_copy(prompt_hbm, prompt_raw.at[own_place], own_sem)
    own_copy.start()
    q_copy = pltpu.make_async_copy(q_hbm, q, q_sem)
    q_copy.start()

    def z_copies(g):
        return (
            remote(near_k.at[g, pl.ds(0, ROWS)], z_k.at[g], z_send.at[2 * g], z_recv.at[2 * g], next_z),
            remote(near_v.at[g, pl.ds(0, ROWS)], z_v.at[g], z_send.at[2 * g + 1], z_recv.at[2 * g + 1], next_z),
        )

    def y_copies(g, k_from, v_from):
        return (
            remote(k_from, y_k.at[g], y_send.at[2 * g], y_recv.at[2 * g], across),
            remote(v_from, y_v.at[g], y_send.at[2 * g + 1], y_recv.at[2 * g + 1], across),
        )

    def own_y_copies(g):
        return y_copies(g, near_k.at[g, pl.ds(0, ROWS)], near_v.at[g, pl.ds(0, ROWS)])

    for g in range(KEY_VALUE_HEADS):
        kv_copies[g].wait()
        both = kv_raw[g].astype(F32)
        near_k[g, 0:ROWS] = both[:, 0].astype(BF16)
        near_v[g, 0:ROWS] = both[:, 1].astype(BF16)
        if g == 0:
            pl.semaphore_wait(barrier, 7)
        for copy in z_copies(g):
            copy.start()

        @pl.when(odd == 0)
        def _():
            for copy in own_y_copies(g):
                copy.start()

    own_copy.wait()
    side_pair = pair + 1 - 2 * lax.rem(pair, 2)
    side_place = pl.ds((core * 8 + side_pair) * 8, 8)
    own_rows = prompt_raw.at[own_place]
    side_rows = prompt_raw.at[side_place]
    first = [
        remote(own_rows, own_rows, first_send.at[k], first_recv.at[k], target)
        for k, target in enumerate((y_side, *x_peers))
    ]
    second = [
        remote(side_rows, side_rows, second_send.at[k], second_recv.at[k], target)
        for k, target in enumerate(x_peers)
    ]
    half = prompt_raw.at[pl.ds(core * 64, 64)]
    third = remote(half, half, third_send, third_recv, sibling)
    for copy in first:
        copy.start()

    slot = slot_ref[c]
    live_length = length_ref[0]
    row = lax.broadcasted_iota(jnp.int32, (ROWS, ROWS), 0)
    column = lax.broadcasted_iota(jnp.int32, (ROWS, ROWS), 1)
    near_ok = (column <= row) & (slot * ROWS + column < live_length)
    near_bias[...] = jnp.where(near_ok, 0.0, NEGATIVE_FILL)

    first[0].wait_recv()
    for copy in second:
        copy.start()
    for copy in (*first[1:], *second):
        copy.wait_recv()
    third.start()
    for copy in (*first, *second):
        copy.wait_send()
    third.wait()
    rows = prompt_raw[...].astype(F32)
    for g in range(KEY_VALUE_HEADS):
        lanes = slice(g * HEAD_SIZE, (g + 1) * HEAD_SIZE)
        near_k[g, ROWS:NEAR] = rows[:, 0, lanes].astype(BF16)
        near_v[g, ROWS:NEAR] = rows[:, 1, lanes].astype(BF16)
    q_copy.wait()

    lane = lax.broadcasted_iota(jnp.int32, (ROWS, HEAD_SIZE), 1)
    ones = jnp.ones((ROWS, HEAD_SIZE), BF16)
    top_all[...] = jnp.zeros_like(top_all)
    total_all[...] = jnp.ones_like(total_all)

    def pipelined(scores, soften, weigh):
        for step in range(GROUP + 2):
            if step < GROUP:
                scores(step)
            if 1 <= step <= GROUP:
                soften(step - 1)
            if step >= 2:
                weigh(step - 2)

    @pl.loop(0, KEY_VALUE_HEADS)
    def _(g):
        def scores(i):
            near_s[i % 2] = lax.dot_general(
                q[:, head_columns(g * GROUP + i)], near_k[g], NT, preferred_element_type=F32
            )

        def soften(i):
            s = near_s[i % 2] * LOG2_SCALE
            s = jnp.concatenate([s[:, :ROWS] + near_bias[...], s[:, ROWS:]], axis=1)
            top = jnp.max(s, axis=1, keepdims=True)
            near_p[i % 2] = jnp.exp2(s - top).astype(BF16)
            near_top[g * GROUP + i] = jnp.broadcast_to(top, (ROWS, HEAD_SIZE))

        def weigh(i):
            v = jnp.concatenate(
                [near_v[g], jnp.ones((NEAR, HEAD_SIZE), BF16)], axis=1
            )
            near_sum[g * GROUP + i] = jnp.dot(near_p[i % 2], v, preferred_element_type=F32)

        pipelined(scores, soften, weigh)

    key = lax.broadcasted_iota(jnp.int32, (1, ROWS), 1)

    def far_bias(back):
        source_slot = slot_ref[lax.rem(c + N_CTX - back, N_CTX)]
        ok = (source_slot * ROWS + key < live_length) & (source_slot < slot)
        return jnp.where(ok, 0.0, NEGATIVE_FILL)

    bias = jnp.concatenate([far_bias(2), far_bias(1)], axis=1)
    query = lax.broadcasted_iota(jnp.int32, (ROWS, HEAD_SIZE), 0)
    is_live = slot * ROWS + query < live_length

    @pl.loop(0, KEY_VALUE_HEADS)
    def _(g):
        forward = y_copies(g, z_k.at[g], z_v.at[g])
        for arriving, onward in zip(z_copies(g), forward, strict=True):
            arriving.wait_recv()

            @pl.when(odd == 1)
            def _():
                onward.start()

        for arriving in forward:
            arriving.wait_recv()

        def scores(i):
            one = q[:, head_columns(g * GROUP + i)]
            far_s[i % 2, :, 0:ROWS] = lax.dot_general(one, z_k[g], NT, preferred_element_type=F32)
            far_s[i % 2, :, ROWS:] = lax.dot_general(one, y_k[g], NT, preferred_element_type=F32)

        def soften(i):
            head = g * GROUP + i
            s = far_s[i % 2] * LOG2_SCALE + bias
            before = near_top[head]
            top = jnp.maximum(before, jnp.max(s, axis=1, keepdims=True))
            far_p[i % 2] = jnp.exp2(s - jnp.concatenate([top] * 4, axis=1)).astype(BF16)
            near_top[head] = jnp.exp2(before - top)
            top_all[...] = jnp.where(lane == head, top, top_all[...])

        def weigh(i):
            head = g * GROUP + i
            v = jnp.concatenate(
                [
                    jnp.concatenate([z_v[g], ones], axis=1),
                    jnp.concatenate([y_v[g], ones], axis=1),
                ],
                axis=0,
            )
            added = jnp.dot(far_p[i % 2], v, preferred_element_type=F32)
            rescale = near_top[head]
            near = near_sum[head]
            total = near[:, HEAD_SIZE:] * rescale + added[:, HEAD_SIZE:]
            summed = near[:, :HEAD_SIZE] * rescale + added[:, :HEAD_SIZE]
            attended = jnp.where(is_live, summed * (1.0 / total), 0.0)
            out_ref[:, head_columns(head)] = attended.astype(BF16)
            total_all[...] = jnp.where(lane == head, total, total_all[...])

        pipelined(scores, soften, weigh)

    log_total = ((top_all[...] + jnp.log2(total_all[...])) * LN2).T[:QUERY_HEADS]
    place = lax.broadcasted_iota(jnp.int32, (QUERY_HEADS, ROWS), 1)
    log_ref[...] = jnp.where(slot * ROWS + place < live_length, log_total, 0.0)

    for g in range(KEY_VALUE_HEADS):
        for copy in (*z_copies(g), *own_y_copies(g)):
            copy.wait_send()


def body(queries, resp_kv, prompt_kv, lengths, block_slot):
    hbm = pl.BlockSpec(memory_space=pltpu.HBM)
    smem = pl.BlockSpec(memory_space=pltpu.SMEM)
    vmem = pl.BlockSpec(memory_space=pltpu.VMEM)
    dma = pltpu.SemaphoreType.DMA
    block = pltpu.VMEM((KEY_VALUE_HEADS, ROWS, HEAD_SIZE), BF16)
    near = pltpu.VMEM((KEY_VALUE_HEADS, NEAR, HEAD_SIZE), BF16)
    attended, log_total = pl.pallas_call(
        kernel,
        out_shape=(
            jax.ShapeDtypeStruct((ROWS, QUERY_HEADS * HEAD_SIZE), BF16),
            jax.ShapeDtypeStruct((QUERY_HEADS, ROWS), F32),
        ),
        in_specs=[hbm, hbm, hbm, smem, smem],
        out_specs=(vmem, vmem),
        scratch_shapes=[
            pltpu.VMEM((ROWS, QUERY_HEADS * HEAD_SIZE), BF16),
            pltpu.VMEM((KEY_VALUE_HEADS, ROWS, 2, HEAD_SIZE), BF16),
            pltpu.VMEM((PROMPT, 2, KEY_VALUE_HEADS * HEAD_SIZE), BF16),
            near, near, block, block, block, block,
            pltpu.VMEM((ROWS, ROWS), F32),
            pltpu.VMEM((QUERY_HEADS, ROWS, HEAD_SIZE), F32),
            pltpu.VMEM((QUERY_HEADS, ROWS, 2 * HEAD_SIZE), F32),
            pltpu.VMEM((ROWS, HEAD_SIZE), F32),
            pltpu.VMEM((ROWS, HEAD_SIZE), F32),
            pltpu.VMEM((2, ROWS, NEAR), F32),
            pltpu.VMEM((2, ROWS, NEAR), BF16),
            pltpu.VMEM((2, ROWS, 2 * ROWS), F32),
            pltpu.VMEM((2, ROWS, 2 * ROWS), BF16),
            dma, dma((4,)), dma, dma((8,)), dma((8,)), dma((8,)), dma((8,)),
            dma((4,)), dma((4,)), dma((3,)), dma((3,)), dma, dma,
        ],
        compiler_params=pltpu.CompilerParams(
            collective_id=0, has_side_effects=True, vmem_limit_bytes=63 * 1024 * 1024
        ),
    )(queries[0], resp_kv[0], prompt_kv[0], lengths, block_slot)
    return attended[None], log_total[None]


def solution(mesh):
    return jax.shard_map(
        body,
        mesh=mesh,
        in_specs=(
            P("resp", "ctx", None),
            P("resp", "ctx", None, None),
            P("ctx", "resp", None, None),
            P("resp"),
            P(),
        ),
        out_specs=(P("resp", "ctx", None), P("resp", None, "ctx")),
        check_vma=False,
    )
```

```python
import math

import jax
import jax.numpy as jnp
from jax import lax
from jax.experimental import pallas as pl
from jax.experimental.pallas import tpu as pltpu
from jax.sharding import PartitionSpec as P

QUERY_HEADS = 32
KEY_VALUE_HEADS = 4
GROUP = QUERY_HEADS // KEY_VALUE_HEADS
HEAD_SIZE = 128
ROWS = 256
PROMPT = 128
LAST = ROWS + PROMPT
N_CTX = 32
N_RESP = 16
NEGATIVE_FILL = -1e30
LOG2_SCALE = math.log2(math.e) / math.sqrt(HEAD_SIZE)
LN2 = math.log(2.0)
F32 = jnp.float32
BF16 = jnp.bfloat16
NT = (((1,), (1,)), ((), ()))
MESH = pl.DeviceIdType.MESH


def at(resp, ctx):
    return {"resp": resp, "ctx": ctx}


def remote(src, dst, send_sem, recv_sem, target):
    return pltpu.make_async_remote_copy(
        src_ref=src,
        dst_ref=dst,
        send_sem=send_sem,
        recv_sem=recv_sem,
        device_id=target,
        device_id_type=MESH,
    )


def head_columns(head):
    return pl.ds(pl.multiple_of(head * HEAD_SIZE, HEAD_SIZE), HEAD_SIZE)


def kernel(
    q_hbm, kv_hbm, prompt_hbm, length_ref, slot_ref,
    out_ref, log_ref,
    q, kv_raw, prompt_raw, own_k, own_v, other_k, other_v,
    near_bias, top_of, sum_of, top_all, total_all, score, weight, out,
    q_sem, kv_sem, own_sem, z_send, z_recv, y_send, y_recv,
    first_send, first_recv, second_send, second_recv, third_send, third_recv, out_sem,
):
    r = lax.axis_index("resp")
    c = lax.axis_index("ctx")
    core = lax.rem(r, 2)
    pair = r // 2
    odd = lax.rem(c, 2)
    next_z = at(r, lax.rem(c + 2, N_CTX))
    prev_z = at(r, lax.rem(c + N_CTX - 2, N_CTX))
    across = at(r, c + 1 - 2 * odd)
    sibling = at(r + 1 - 2 * core, c)
    y_side = at(r + 2 - 4 * lax.rem(pair, 2), c)
    x_peers = [at(lax.rem(r + 4 * k, N_RESP), c) for k in (1, 2, 3)]

    barrier = pltpu.get_barrier_semaphore()
    for device in (prev_z, across, sibling, y_side, *x_peers):
        pl.semaphore_signal(barrier, inc=1, device_id=device, device_id_type=MESH)

    kv_copies = [
        pltpu.make_async_copy(
            kv_hbm.at[:, :, pl.ds(g * HEAD_SIZE, HEAD_SIZE)], kv_raw.at[g], kv_sem.at[g]
        )
        for g in range(KEY_VALUE_HEADS)
    ]
    for copy in kv_copies:
        copy.start()
    own_place = pl.ds((core * 8 + pair) * 8, 8)
    own_copy = pltpu.make_async_copy(prompt_hbm, prompt_raw.at[own_place], own_sem)
    own_copy.start()
    q_copy = pltpu.make_async_copy(q_hbm, q, q_sem)
    q_copy.start()

    def pieces(k_from, v_from, slot_of, g, sends, receives, target):
        places = pl.ds(0, ROWS)
        return (
            remote(k_from, other_k.at[slot_of, g, places], sends.at[2 * g], receives.at[2 * g], target),
            remote(v_from, other_v.at[slot_of, g, places], sends.at[2 * g + 1], receives.at[2 * g + 1], target),
        )

    def z_copies(g):
        return pieces(own_k.at[g], own_v.at[g], odd, g, z_send, z_recv, next_z)

    def own_y_copies(g):
        return pieces(own_k.at[g], own_v.at[g], 0, g, y_send, y_recv, across)

    def onward_copies(g):
        k_from = other_k.at[1, g, pl.ds(0, ROWS)]
        v_from = other_v.at[1, g, pl.ds(0, ROWS)]
        return pieces(k_from, v_from, 1, g, y_send, y_recv, across)

    side_pair = pair + 1 - 2 * lax.rem(pair, 2)
    side_place = pl.ds((core * 8 + side_pair) * 8, 8)
    own_rows = prompt_raw.at[own_place]
    side_rows = prompt_raw.at[side_place]
    first = [
        remote(prompt_hbm, own_rows, first_send.at[k], first_recv.at[k], target)
        for k, target in enumerate((y_side, *x_peers))
    ]
    second = [
        remote(side_rows, side_rows, second_send.at[k], second_recv.at[k], target)
        for k, target in enumerate(x_peers)
    ]
    half = prompt_raw.at[pl.ds(core * 64, 64)]
    third = remote(half, half, third_send, third_recv, sibling)

    for g in range(KEY_VALUE_HEADS):
        kv_copies[g].wait()
        both = kv_raw[g].astype(F32)
        own_k[g] = both[:, 0].astype(BF16)
        own_v[g] = both[:, 1].astype(BF16)
        if g == 0:
            pl.semaphore_wait(barrier, 7)
        for copy in z_copies(g):
            copy.start()

        @pl.when(odd == 0)
        def _():
            for copy in own_y_copies(g):
                copy.start()

        if g == 0:
            for copy in first:
                copy.start()

    slot = slot_ref[c]
    live_length = length_ref[0]
    row = lax.broadcasted_iota(jnp.int32, (ROWS, ROWS), 0)
    column = lax.broadcasted_iota(jnp.int32, (ROWS, ROWS), 1)
    near_ok = (column <= row) & (slot * ROWS + column < live_length)
    near_bias[...] = jnp.where(near_ok, 0.0, NEGATIVE_FILL)
    key = lax.broadcasted_iota(jnp.int32, (1, ROWS), 1)

    def other_bias(back):
        source_slot = slot_ref[lax.rem(c + N_CTX - back, N_CTX)]
        ok = (source_slot * ROWS + key < live_length) & (source_slot < slot)
        return jnp.where(ok, 0.0, NEGATIVE_FILL)

    early_bias = jnp.concatenate([other_bias(2 - odd), jnp.zeros((1, PROMPT), F32)], axis=1)
    late_bias = other_bias(1 + odd)
    query = lax.broadcasted_iota(jnp.int32, (ROWS, HEAD_SIZE), 0)
    is_live = slot * ROWS + query < live_length
    lane = lax.broadcasted_iota(jnp.int32, (ROWS, HEAD_SIZE), 1)
    top_all[...] = jnp.zeros_like(top_all)
    total_all[...] = jnp.ones_like(total_all)

    def absorb(g, k_ref, v_ref, width, bias, is_first, is_last):
        k_tile = k_ref.at[g, pl.ds(0, width)]
        v_tile = v_ref.at[g, pl.ds(0, width)]

        def scores(i):
            score[i % 2, :, 0:width] = lax.dot_general(
                q[:, head_columns(g * GROUP + i)], k_tile[...], NT, preferred_element_type=F32
            )

        def soften(i):
            head = g * GROUP + i
            s = score[i % 2, :, 0:width] * LOG2_SCALE + bias()
            peak = jnp.max(s, axis=1, keepdims=True)
            if is_first:
                top = jnp.broadcast_to(peak, (ROWS, HEAD_SIZE))
            else:
                before = top_of[0, head]
                top = jnp.maximum(before, peak)
                top_of[1, head] = jnp.exp2(before - top)
            top_of[0, head] = top
            shift = jnp.concatenate([top] * (width // HEAD_SIZE), axis=1)
            weight[i % 2, :, 0:width] = jnp.exp2(s - shift).astype(BF16)
            if is_last:
                top_all[...] = jnp.where(lane == head, top, top_all[...])

        def weigh(i):
            head = g * GROUP + i
            v = jnp.concatenate([v_tile[...], jnp.ones((width, HEAD_SIZE), BF16)], axis=1)
            added = jnp.dot(weight[i % 2, :, 0:width], v, preferred_element_type=F32)
            if is_first:
                sum_of[head] = added
                return
            rescale = top_of[1, head]
            held = sum_of[head]
            summed = held[:, :HEAD_SIZE] * rescale + added[:, :HEAD_SIZE]
            total = held[:, HEAD_SIZE:] * rescale + added[:, HEAD_SIZE:]
            if not is_last:
                sum_of[head, :, 0:HEAD_SIZE] = summed
                sum_of[head, :, HEAD_SIZE:] = total
                return
            attended = jnp.where(is_live, summed * (1.0 / total), 0.0)
            out[:, head_columns(head)] = attended.astype(BF16)
            total_all[...] = jnp.where(lane == head, total, total_all[...])

        for step in range(GROUP + 2):
            if step < GROUP:
                scores(step)
            if 1 <= step <= GROUP:
                soften(step - 1)
            if step >= 2:
                weigh(step - 2)

    q_copy.wait()
    first[0].wait_recv()
    for copy in second:
        copy.start()

    @pl.loop(0, KEY_VALUE_HEADS)
    def _(g):
        absorb(g, own_k, own_v, ROWS, lambda: near_bias[...], True, False)

    def out_copy(g):
        wide = GROUP * HEAD_SIZE
        columns = pl.ds(pl.multiple_of(g * wide, wide), wide)
        return pltpu.make_async_copy(out.at[:, columns], out_ref.at[:, columns], out_sem.at[g])

    own_copy.wait()
    for copy in (*first[1:], *second):
        copy.wait_recv()
    third.start()
    for copy in (*first, *second):
        copy.wait_send()
    third.wait()
    rows = prompt_raw[...].astype(F32)
    for g in range(KEY_VALUE_HEADS):
        lanes = slice(g * HEAD_SIZE, (g + 1) * HEAD_SIZE)
        other_k[0, g, ROWS:LAST] = rows[:, 0, lanes].astype(BF16)
        other_v[0, g, ROWS:LAST] = rows[:, 1, lanes].astype(BF16)

    @pl.loop(0, KEY_VALUE_HEADS)
    def _(g):
        @pl.when(odd == 0)
        def _():
            for arriving in z_copies(g):
                arriving.wait_recv()

        @pl.when(odd == 1)
        def _():
            for arriving in own_y_copies(g):
                arriving.wait_recv()

        absorb(g, other_k.at[0], other_v.at[0], LAST, lambda: early_bias, False, False)

        @pl.when(odd == 0)
        def _():
            for arriving in onward_copies(g):
                arriving.wait_recv()

        @pl.when(odd == 1)
        def _():
            for arriving, sending in zip(z_copies(g), onward_copies(g), strict=True):
                arriving.wait_recv()
                sending.start()

        absorb(g, other_k.at[1], other_v.at[1], ROWS, lambda: late_bias, False, True)
        out_copy(g).start()

    log_total = ((top_all[...] + jnp.log2(total_all[...])) * LN2).T[:QUERY_HEADS]
    place = lax.broadcasted_iota(jnp.int32, (QUERY_HEADS, ROWS), 1)
    log_ref[...] = jnp.where(slot * ROWS + place < live_length, log_total, 0.0)

    for g in range(KEY_VALUE_HEADS):
        for copy in (*z_copies(g), *own_y_copies(g)):
            copy.wait_send()
        out_copy(g).wait()


def hand_on(attended_in, log_in, attended_out, log_out, held, held_log, in_sem, out_sem):
    pieces = 8
    rows = ROWS // pieces
    places = [pl.ds(i * rows, rows) for i in range(pieces)]
    inward = [pltpu.make_async_copy(attended_in.at[p], held.at[p], in_sem.at[i]) for i, p in enumerate(places)]
    outward = [pltpu.make_async_copy(held.at[p], attended_out.at[p], out_sem.at[i]) for i, p in enumerate(places)]
    inward.append(pltpu.make_async_copy(log_in, held_log, in_sem.at[pieces]))
    outward.append(pltpu.make_async_copy(held_log, log_out, out_sem.at[pieces]))
    for copy in inward:
        copy.start()
    for arriving, leaving in zip(inward, outward, strict=True):
        arriving.wait()
        leaving.start()
    for leaving in outward:
        leaving.wait()


def body(queries, resp_kv, prompt_kv, lengths, block_slot):
    hbm = pl.BlockSpec(memory_space=pltpu.HBM)
    smem = pl.BlockSpec(memory_space=pltpu.SMEM)
    vmem = pl.BlockSpec(memory_space=pltpu.VMEM)
    dma = pltpu.SemaphoreType.DMA
    block = pltpu.VMEM((KEY_VALUE_HEADS, ROWS, HEAD_SIZE), BF16)
    other = pltpu.VMEM((2, KEY_VALUE_HEADS, LAST, HEAD_SIZE), BF16)
    attended, log_total = pl.pallas_call(
        kernel,
        out_shape=(
            jax.ShapeDtypeStruct((ROWS, QUERY_HEADS * HEAD_SIZE), BF16),
            jax.ShapeDtypeStruct((QUERY_HEADS, ROWS), F32),
        ),
        in_specs=[hbm, hbm, hbm, smem, smem],
        out_specs=(hbm, vmem),
        scratch_shapes=[
            pltpu.VMEM((ROWS, QUERY_HEADS * HEAD_SIZE), BF16),
            pltpu.VMEM((KEY_VALUE_HEADS, ROWS, 2, HEAD_SIZE), BF16),
            pltpu.VMEM((PROMPT, 2, KEY_VALUE_HEADS * HEAD_SIZE), BF16),
            block, block, other, other,
            pltpu.VMEM((ROWS, ROWS), F32),
            pltpu.VMEM((2, QUERY_HEADS, ROWS, HEAD_SIZE), F32),
            pltpu.VMEM((QUERY_HEADS, ROWS, 2 * HEAD_SIZE), F32),
            pltpu.VMEM((ROWS, HEAD_SIZE), F32),
            pltpu.VMEM((ROWS, HEAD_SIZE), F32),
            pltpu.VMEM((2, ROWS, LAST), F32),
            pltpu.VMEM((2, ROWS, LAST), BF16),
            pltpu.VMEM((ROWS, QUERY_HEADS * HEAD_SIZE), BF16),
            dma, dma((4,)), dma, dma((8,)), dma((8,)), dma((8,)), dma((8,)),
            dma((4,)), dma((4,)), dma((3,)), dma((3,)), dma, dma, dma((4,)),
        ],
        compiler_params=pltpu.CompilerParams(
            collective_id=0, has_side_effects=True, vmem_limit_bytes=63 * 1024 * 1024
        ),
    )(queries[0], resp_kv[0], prompt_kv[0], lengths, block_slot)
    attended, log_total = pl.pallas_call(
        hand_on,
        out_shape=(
            jax.ShapeDtypeStruct((ROWS, QUERY_HEADS * HEAD_SIZE), BF16),
            jax.ShapeDtypeStruct((QUERY_HEADS, ROWS), F32),
        ),
        in_specs=[hbm, hbm],
        out_specs=(hbm, hbm),
        scratch_shapes=[
            pltpu.VMEM((ROWS, QUERY_HEADS * HEAD_SIZE), BF16),
            pltpu.VMEM((QUERY_HEADS, ROWS), F32),
            dma((9,)), dma((9,)),
        ],
        compiler_params=pltpu.CompilerParams(vmem_limit_bytes=63 * 1024 * 1024),
    )(attended, log_total)
    return attended[None], log_total[None]


def solution(mesh):
    return jax.shard_map(
        body,
        mesh=mesh,
        in_specs=(
            P("resp", "ctx", None),
            P("resp", "ctx", None, None),
            P("ctx", "resp", None, None),
            P("resp"),
            P(),
        ),
        out_specs=(P("resp", "ctx", None), P("resp", None, "ctx")),
        check_vma=False,
    )
```

```python
import math

import jax
import jax.numpy as jnp
from jax import lax
from jax.experimental import pallas as pl
from jax.experimental.pallas import tpu as pltpu
from jax.sharding import PartitionSpec as P

QUERY_HEADS = 32
KEY_VALUE_HEADS = 4
GROUP = QUERY_HEADS // KEY_VALUE_HEADS
HEAD_SIZE = 128
ROWS = 256
PROMPT = 128
LAST = ROWS + PROMPT
N_CTX = 32
AHEAD = 2
N_RESP = 16
NEGATIVE_FILL = -1e30
LOG2_SCALE = math.log2(math.e) / math.sqrt(HEAD_SIZE)
LN2 = math.log(2.0)
F32 = jnp.float32
BF16 = jnp.bfloat16
NT = (((1,), (1,)), ((), ()))
MESH = pl.DeviceIdType.MESH


def at(resp, ctx):
    return {"resp": resp, "ctx": ctx}


def remote(src, dst, send_sem, recv_sem, target):
    return pltpu.make_async_remote_copy(
        src_ref=src,
        dst_ref=dst,
        send_sem=send_sem,
        recv_sem=recv_sem,
        device_id=target,
        device_id_type=MESH,
    )


def head_columns(head):
    return pl.ds(pl.multiple_of(head * HEAD_SIZE, HEAD_SIZE), HEAD_SIZE)


def kernel(
    q_hbm, kv_hbm, prompt_hbm, length_ref, slot_ref,
    out_ref, log_ref,
    q, kv_raw, prompt_raw, own_k, own_v, other_k, other_v,
    near_bias, top_of, sum_of, top_all, total_all, score, weight, out,
    q_sem, kv_sem, own_sem, z_send, z_recv, y_send, y_recv,
    first_send, first_recv, second_send, second_recv, third_send, third_recv, out_sem,
):
    r = lax.axis_index("resp")
    c = lax.axis_index("ctx")
    core = lax.rem(r, 2)
    pair = r // 2
    odd = lax.rem(c, 2)
    next_z = at(r, lax.rem(c + 2, N_CTX))
    prev_z = at(r, lax.rem(c + N_CTX - 2, N_CTX))
    across = at(r, c + 1 - 2 * odd)
    sibling = at(r + 1 - 2 * core, c)
    y_side = at(r + 2 - 4 * lax.rem(pair, 2), c)
    x_peers = [at(lax.rem(r + 4 * k, N_RESP), c) for k in (1, 2, 3)]

    barrier = pltpu.get_barrier_semaphore()
    for device in (prev_z, across, sibling, y_side, *x_peers):
        pl.semaphore_signal(barrier, inc=1, device_id=device, device_id_type=MESH)

    kv_copies = [
        pltpu.make_async_copy(
            kv_hbm.at[:, :, pl.ds(g * HEAD_SIZE, HEAD_SIZE)], kv_raw.at[g], kv_sem.at[g]
        )
        for g in range(KEY_VALUE_HEADS)
    ]
    for copy in kv_copies:
        copy.start()
    own_place = pl.ds((core * 8 + pair) * 8, 8)
    own_copy = pltpu.make_async_copy(prompt_hbm, prompt_raw.at[own_place], own_sem)
    own_copy.start()
    q_copy = pltpu.make_async_copy(q_hbm, q, q_sem)
    q_copy.start()

    def pieces(k_from, v_from, slot_of, g, sends, receives, target):
        places = pl.ds(0, ROWS)
        return (
            remote(k_from, other_k.at[slot_of, g, places], sends.at[2 * g], receives.at[2 * g], target),
            remote(v_from, other_v.at[slot_of, g, places], sends.at[2 * g + 1], receives.at[2 * g + 1], target),
        )

    def z_copies(g):
        return pieces(own_k.at[g], own_v.at[g], odd, g, z_send, z_recv, next_z)

    def own_y_copies(g):
        return pieces(own_k.at[g], own_v.at[g], 0, g, y_send, y_recv, across)

    def onward_copies(g):
        k_from = other_k.at[1, g, pl.ds(0, ROWS)]
        v_from = other_v.at[1, g, pl.ds(0, ROWS)]
        return pieces(k_from, v_from, 1, g, y_send, y_recv, across)

    side_pair = pair + 1 - 2 * lax.rem(pair, 2)
    side_place = pl.ds((core * 8 + side_pair) * 8, 8)
    own_rows = prompt_raw.at[own_place]
    side_rows = prompt_raw.at[side_place]
    first = [
        remote(prompt_hbm, own_rows, first_send.at[k], first_recv.at[k], target)
        for k, target in enumerate((y_side, *x_peers))
    ]
    second = [
        remote(side_rows, side_rows, second_send.at[k], second_recv.at[k], target)
        for k, target in enumerate(x_peers)
    ]
    half = prompt_raw.at[pl.ds(core * 64, 64)]
    third = remote(half, half, third_send, third_recv, sibling)

    for g in range(KEY_VALUE_HEADS):
        kv_copies[g].wait()
        both = kv_raw[g].astype(F32)
        own_k[g] = both[:, 0].astype(BF16)
        own_v[g] = both[:, 1].astype(BF16)
        if g == 0:
            pl.semaphore_wait(barrier, 7)
        for copy in z_copies(g):
            copy.start()

        if g == 0:
            for copy in first:
                copy.start()

    @pl.when(odd == 0)
    def _():
        for g in range(KEY_VALUE_HEADS):
            for copy in own_y_copies(g):
                copy.start()

    slot = slot_ref[c]
    live_length = length_ref[0]
    row = lax.broadcasted_iota(jnp.int32, (ROWS, ROWS), 0)
    column = lax.broadcasted_iota(jnp.int32, (ROWS, ROWS), 1)
    near_ok = (column <= row) & (slot * ROWS + column < live_length)
    near_bias[...] = jnp.where(near_ok, 0.0, NEGATIVE_FILL)
    key = lax.broadcasted_iota(jnp.int32, (1, ROWS), 1)

    def other_bias(back):
        source_slot = slot_ref[lax.rem(c + N_CTX - back, N_CTX)]
        ok = (source_slot * ROWS + key < live_length) & (source_slot < slot)
        return jnp.where(ok, 0.0, NEGATIVE_FILL)

    early_bias = jnp.concatenate([other_bias(2 - odd), jnp.zeros((1, PROMPT), F32)], axis=1)
    late_bias = other_bias(1 + odd)
    query = lax.broadcasted_iota(jnp.int32, (ROWS, HEAD_SIZE), 0)
    is_live = slot * ROWS + query < live_length
    lane = lax.broadcasted_iota(jnp.int32, (ROWS, HEAD_SIZE), 1)
    top_all[...] = jnp.zeros_like(top_all)
    total_all[...] = jnp.ones_like(total_all)

    def absorb(g, k_ref, v_ref, width, bias, is_first, is_last, await_values=None):
        held_heads = GROUP if is_last else 2
        k_tile = k_ref.at[g, pl.ds(0, width)]
        v_tile = v_ref.at[g, pl.ds(0, width)]

        def scores(i):
            score[i % 2, :, 0:width] = lax.dot_general(
                q[:, head_columns(g * GROUP + i)], k_tile[...], NT, preferred_element_type=F32
            )

        def soften(i):
            head = g * GROUP + i
            s = score[i % 2, :, 0:width] * LOG2_SCALE + bias()
            peak = jnp.max(s, axis=1, keepdims=True)
            if is_first:
                top = jnp.broadcast_to(peak, (ROWS, HEAD_SIZE))
            else:
                before = top_of[0, head]
                top = jnp.maximum(before, peak)
                top_of[1, head] = jnp.exp2(before - top)
            top_of[0, head] = top
            shift = jnp.concatenate([top] * (width // HEAD_SIZE), axis=1)
            weight[i % held_heads, :, 0:width] = jnp.exp2(s - shift).astype(BF16)
            if is_last:
                top_all[...] = jnp.where(lane == head, top, top_all[...])

        def weigh(i):
            head = g * GROUP + i
            v = jnp.concatenate([v_tile[...], jnp.ones((width, HEAD_SIZE), BF16)], axis=1)
            added = jnp.dot(weight[i % held_heads, :, 0:width], v, preferred_element_type=F32)
            if is_first:
                sum_of[head] = added
                return
            rescale = top_of[1, head]
            held = sum_of[head]
            summed = held[:, :HEAD_SIZE] * rescale + added[:, :HEAD_SIZE]
            total = held[:, HEAD_SIZE:] * rescale + added[:, HEAD_SIZE:]
            if not is_last:
                sum_of[head, :, 0:HEAD_SIZE] = summed
                sum_of[head, :, HEAD_SIZE:] = total
                return
            attended = jnp.where(is_live, summed * (1.0 / total), 0.0)
            out[:, head_columns(head)] = attended.astype(BF16)
            total_all[...] = jnp.where(lane == head, total, total_all[...])

        if is_last:
            for step in range(GROUP + 1):
                if step < GROUP:
                    scores(step)
                if step >= 1:
                    soften(step - 1)
            await_values()
            for step in range(GROUP):
                weigh(step)
            return
        for step in range(GROUP + 2):
            if step < GROUP:
                scores(step)
            if 1 <= step <= GROUP:
                soften(step - 1)
            if step >= 2:
                weigh(step - 2)

    q_copy.wait()
    first[0].wait_recv()
    for copy in second:
        copy.start()

    @pl.loop(0, KEY_VALUE_HEADS)
    def _(g):
        absorb(g, own_k, own_v, ROWS, lambda: near_bias[...], True, False)

    def out_copy(g):
        wide = GROUP * HEAD_SIZE
        columns = pl.ds(pl.multiple_of(g * wide, wide), wide)
        return pltpu.make_async_copy(out.at[:, columns], out_ref.at[:, columns], out_sem.at[g])

    def pass_on(g):
        @pl.when((odd == 1) & (c >= 2))
        def _():
            for arriving, sending in zip(z_copies(g), onward_copies(g), strict=True):
                arriving.wait_recv()
                sending.start()

    pass_on(0)
    own_copy.wait()
    for copy in (*first[1:], *second):
        copy.wait_recv()
    third.start()
    pass_on(1)
    for copy in (*first, *second):
        copy.wait_send()
    third.wait()
    rows = prompt_raw[...].astype(F32)
    for g in range(KEY_VALUE_HEADS):
        lanes = slice(g * HEAD_SIZE, (g + 1) * HEAD_SIZE)
        other_k[0, g, ROWS:LAST] = rows[:, 0, lanes].astype(BF16)
        other_v[0, g, ROWS:LAST] = rows[:, 1, lanes].astype(BF16)

    @pl.loop(0, KEY_VALUE_HEADS)
    def _(g):
        @pl.when(odd == 0)
        def _():
            for arriving in z_copies(g):
                arriving.wait_recv()

        @pl.when(odd == 1)
        def _():
            for arriving in own_y_copies(g):
                arriving.wait_recv()

        absorb(g, other_k.at[0], other_v.at[0], LAST, lambda: early_bias, False, False)

        arriving_far = z_copies(g)
        passing = onward_copies(g)

        def await_part(part):
            @pl.when(odd == 0)
            def _():
                passing[part].wait_recv()

            @pl.when((odd == 1) & ((c < 2) | (g >= AHEAD)))
            def _():
                arriving_far[part].wait_recv()
                passing[part].start()

        await_part(0)
        absorb(
            g, other_k.at[1], other_v.at[1], ROWS, lambda: late_bias, False, True, lambda: await_part(1)
        )
        out_copy(g).start()

    log_total = ((top_all[...] + jnp.log2(total_all[...])) * LN2).T[:QUERY_HEADS]
    place = lax.broadcasted_iota(jnp.int32, (QUERY_HEADS, ROWS), 1)
    log_ref[...] = jnp.where(slot * ROWS + place < live_length, log_total, 0.0)

    for g in range(KEY_VALUE_HEADS):
        for copy in (*z_copies(g), *own_y_copies(g)):
            copy.wait_send()
        out_copy(g).wait()


def hand_on(attended_in, log_in, attended_out, log_out, held, held_log, in_sem, out_sem):
    pieces = 8
    rows = ROWS // pieces
    places = [pl.ds(i * rows, rows) for i in range(pieces)]
    inward = [pltpu.make_async_copy(attended_in.at[p], held.at[p], in_sem.at[i]) for i, p in enumerate(places)]
    outward = [pltpu.make_async_copy(held.at[p], attended_out.at[p], out_sem.at[i]) for i, p in enumerate(places)]
    inward.append(pltpu.make_async_copy(log_in, held_log, in_sem.at[pieces]))
    outward.append(pltpu.make_async_copy(held_log, log_out, out_sem.at[pieces]))
    for copy in inward:
        copy.start()
    for arriving, leaving in zip(inward, outward, strict=True):
        arriving.wait()
        leaving.start()
    for leaving in outward:
        leaving.wait()


def body(queries, resp_kv, prompt_kv, lengths, block_slot):
    hbm = pl.BlockSpec(memory_space=pltpu.HBM)
    smem = pl.BlockSpec(memory_space=pltpu.SMEM)
    vmem = pl.BlockSpec(memory_space=pltpu.VMEM)
    dma = pltpu.SemaphoreType.DMA
    block = pltpu.VMEM((KEY_VALUE_HEADS, ROWS, HEAD_SIZE), BF16)
    other = pltpu.VMEM((2, KEY_VALUE_HEADS, LAST, HEAD_SIZE), BF16)
    attended, log_total = pl.pallas_call(
        kernel,
        out_shape=(
            jax.ShapeDtypeStruct((ROWS, QUERY_HEADS * HEAD_SIZE), BF16),
            jax.ShapeDtypeStruct((QUERY_HEADS, ROWS), F32),
        ),
        in_specs=[hbm, hbm, hbm, smem, smem],
        out_specs=(hbm, vmem),
        scratch_shapes=[
            pltpu.VMEM((ROWS, QUERY_HEADS * HEAD_SIZE), BF16),
            pltpu.VMEM((KEY_VALUE_HEADS, ROWS, 2, HEAD_SIZE), BF16),
            pltpu.VMEM((PROMPT, 2, KEY_VALUE_HEADS * HEAD_SIZE), BF16),
            block, block, other, other,
            pltpu.VMEM((ROWS, ROWS), F32),
            pltpu.VMEM((2, QUERY_HEADS, ROWS, HEAD_SIZE), F32),
            pltpu.VMEM((QUERY_HEADS, ROWS, 2 * HEAD_SIZE), F32),
            pltpu.VMEM((ROWS, HEAD_SIZE), F32),
            pltpu.VMEM((ROWS, HEAD_SIZE), F32),
            pltpu.VMEM((2, ROWS, LAST), F32),
            pltpu.VMEM((GROUP, ROWS, LAST), BF16),
            pltpu.VMEM((ROWS, QUERY_HEADS * HEAD_SIZE), BF16),
            dma, dma((4,)), dma, dma((8,)), dma((8,)), dma((8,)), dma((8,)),
            dma((4,)), dma((4,)), dma((3,)), dma((3,)), dma, dma, dma((4,)),
        ],
        compiler_params=pltpu.CompilerParams(
            collective_id=0, has_side_effects=True, vmem_limit_bytes=63 * 1024 * 1024
        ),
    )(queries[0], resp_kv[0], prompt_kv[0], lengths, block_slot)
    attended, log_total = pl.pallas_call(
        hand_on,
        out_shape=(
            jax.ShapeDtypeStruct((ROWS, QUERY_HEADS * HEAD_SIZE), BF16),
            jax.ShapeDtypeStruct((QUERY_HEADS, ROWS), F32),
        ),
        in_specs=[hbm, hbm],
        out_specs=(hbm, hbm),
        scratch_shapes=[
            pltpu.VMEM((ROWS, QUERY_HEADS * HEAD_SIZE), BF16),
            pltpu.VMEM((QUERY_HEADS, ROWS), F32),
            dma((9,)), dma((9,)),
        ],
        compiler_params=pltpu.CompilerParams(vmem_limit_bytes=63 * 1024 * 1024),
    )(attended, log_total)
    return attended[None], log_total[None]


def solution(mesh):
    return jax.shard_map(
        body,
        mesh=mesh,
        in_specs=(
            P("resp", "ctx", None),
            P("resp", "ctx", None, None),
            P("ctx", "resp", None, None),
            P("resp"),
            P(),
        ),
        out_specs=(P("resp", "ctx", None), P("resp", None, "ctx")),
        check_vma=False,
    )
```

```python
import math

import jax
import jax.numpy as jnp
from jax import lax
from jax.experimental import pallas as pl
from jax.experimental.pallas import tpu as pltpu
from jax.sharding import PartitionSpec as P

QUERY_HEADS = 32
KEY_VALUE_HEADS = 4
GROUP = QUERY_HEADS // KEY_VALUE_HEADS
HEAD_SIZE = 128
ROWS = 256
PROMPT = 128
LAST = ROWS + PROMPT
N_CTX = 32
AHEAD = 2
N_RESP = 16
NEGATIVE_FILL = -1e30
LOG2_SCALE = math.log2(math.e) / math.sqrt(HEAD_SIZE)
LN2 = math.log(2.0)
F32 = jnp.float32
BF16 = jnp.bfloat16
NT = (((1,), (1,)), ((), ()))
MESH = pl.DeviceIdType.MESH


def at(resp, ctx):
    return {"resp": resp, "ctx": ctx}


def remote(src, dst, send_sem, recv_sem, target):
    return pltpu.make_async_remote_copy(
        src_ref=src,
        dst_ref=dst,
        send_sem=send_sem,
        recv_sem=recv_sem,
        device_id=target,
        device_id_type=MESH,
    )


def head_columns(head):
    return pl.ds(pl.multiple_of(head * HEAD_SIZE, HEAD_SIZE), HEAD_SIZE)


def kernel(
    q_hbm, kv_hbm, prompt_hbm, length_ref, slot_ref,
    out_ref, log_ref,
    q, kv_raw, prompt_raw, own_k, own_v, other_k, other_v,
    near_bias, top_of, sum_of, top_all, total_all, score, weight, out,
    q_sem, kv_sem, own_sem, z_send, z_recv, y_send, y_recv,
    first_send, first_recv, second_send, second_recv, third_send, third_recv, out_sem,
):
    r = lax.axis_index("resp")
    c = lax.axis_index("ctx")
    core = lax.rem(r, 2)
    pair = r // 2
    odd = lax.rem(c, 2)
    next_z = at(r, lax.rem(c + 2, N_CTX))
    prev_z = at(r, lax.rem(c + N_CTX - 2, N_CTX))
    across = at(r, c + 1 - 2 * odd)
    sibling = at(r + 1 - 2 * core, c)
    y_side = at(r + 2 - 4 * lax.rem(pair, 2), c)
    x_peers = [at(lax.rem(r + 4 * k, N_RESP), c) for k in (1, 2, 3)]

    barrier = pltpu.get_barrier_semaphore()
    for device in (prev_z, across, sibling, y_side, *x_peers):
        pl.semaphore_signal(barrier, inc=1, device_id=device, device_id_type=MESH)

    kv_copies = [
        pltpu.make_async_copy(
            kv_hbm.at[:, :, pl.ds(g * HEAD_SIZE, HEAD_SIZE)], kv_raw.at[g], kv_sem.at[g]
        )
        for g in range(KEY_VALUE_HEADS)
    ]
    for copy in kv_copies:
        copy.start()
    own_place = pl.ds((core * 8 + pair) * 8, 8)
    own_copy = pltpu.make_async_copy(prompt_hbm, prompt_raw.at[own_place], own_sem)
    own_copy.start()
    q_copy = pltpu.make_async_copy(q_hbm, q, q_sem)
    q_copy.start()

    def pieces(k_from, v_from, slot_of, g, sends, receives, target):
        parts = [(k_from, other_k.at[slot_of, g, pl.ds(0, ROWS)])]
        for start in (0, ROWS // 2):
            places = pl.ds(start, ROWS // 2)
            parts.append((v_from.at[places], other_v.at[slot_of, g, places]))
        return tuple(
            remote(src, dst, sends.at[3 * g + k], receives.at[3 * g + k], target)
            for k, (src, dst) in enumerate(parts)
        )

    def z_copies(g):
        return pieces(own_k.at[g], own_v.at[g], odd, g, z_send, z_recv, next_z)

    def own_y_copies(g):
        return pieces(own_k.at[g], own_v.at[g], 0, g, y_send, y_recv, across)

    def onward_copies(g):
        k_from = other_k.at[1, g, pl.ds(0, ROWS)]
        v_from = other_v.at[1, g, pl.ds(0, ROWS)]
        return pieces(k_from, v_from, 1, g, y_send, y_recv, across)

    side_pair = pair + 1 - 2 * lax.rem(pair, 2)
    side_place = pl.ds((core * 8 + side_pair) * 8, 8)
    own_rows = prompt_raw.at[own_place]
    side_rows = prompt_raw.at[side_place]
    first = [
        remote(prompt_hbm, own_rows, first_send.at[k], first_recv.at[k], target)
        for k, target in enumerate((y_side, *x_peers))
    ]
    second = [
        remote(side_rows, side_rows, second_send.at[k], second_recv.at[k], target)
        for k, target in enumerate(x_peers)
    ]
    half = prompt_raw.at[pl.ds(core * 64, 64)]
    third = remote(half, half, third_send, third_recv, sibling)

    for g in range(KEY_VALUE_HEADS):
        kv_copies[g].wait()
        both = kv_raw[g].astype(F32)
        own_k[g] = both[:, 0].astype(BF16)
        own_v[g] = both[:, 1].astype(BF16)
        if g == 0:
            pl.semaphore_wait(barrier, 7)
        for copy in z_copies(g):
            copy.start()

        if g == 0:
            for copy in first:
                copy.start()

    @pl.when(odd == 0)
    def _():
        for g in range(KEY_VALUE_HEADS):
            for copy in own_y_copies(g):
                copy.start()

    slot = slot_ref[c]
    live_length = length_ref[0]
    row = lax.broadcasted_iota(jnp.int32, (ROWS, ROWS), 0)
    column = lax.broadcasted_iota(jnp.int32, (ROWS, ROWS), 1)
    near_ok = (column <= row) & (slot * ROWS + column < live_length)
    near_bias[...] = jnp.where(near_ok, 0.0, NEGATIVE_FILL)
    key = lax.broadcasted_iota(jnp.int32, (1, ROWS), 1)

    def other_bias(back):
        source_slot = slot_ref[lax.rem(c + N_CTX - back, N_CTX)]
        ok = (source_slot * ROWS + key < live_length) & (source_slot < slot)
        return jnp.where(ok, 0.0, NEGATIVE_FILL)

    early_bias = jnp.concatenate([other_bias(2 - odd), jnp.zeros((1, PROMPT), F32)], axis=1)
    late_bias = other_bias(1 + odd)
    query = lax.broadcasted_iota(jnp.int32, (ROWS, HEAD_SIZE), 0)
    is_live = slot * ROWS + query < live_length
    lane = lax.broadcasted_iota(jnp.int32, (ROWS, HEAD_SIZE), 1)
    top_all[...] = jnp.zeros_like(top_all)
    total_all[...] = jnp.ones_like(total_all)

    def absorb(g, k_ref, v_ref, width, bias, is_first, is_last, await_values=None):
        held_heads = GROUP if is_last else 2
        k_tile = k_ref.at[g, pl.ds(0, width)]
        v_tile = v_ref.at[g, pl.ds(0, width)]

        def scores(i):
            score[i % 2, :, 0:width] = lax.dot_general(
                q[:, head_columns(g * GROUP + i)], k_tile[...], NT, preferred_element_type=F32
            )

        def soften(i):
            head = g * GROUP + i
            s = score[i % 2, :, 0:width] * LOG2_SCALE + bias()
            peak = jnp.max(s, axis=1, keepdims=True)
            if is_first:
                top = jnp.broadcast_to(peak, (ROWS, HEAD_SIZE))
            else:
                before = top_of[0, head]
                top = jnp.maximum(before, peak)
                top_of[1, head] = jnp.exp2(before - top)
            top_of[0, head] = top
            shift = jnp.concatenate([top] * (width // HEAD_SIZE), axis=1)
            weight[i % held_heads, :, 0:width] = jnp.exp2(s - shift).astype(BF16)
            if is_last:
                top_all[...] = jnp.where(lane == head, top, top_all[...])

        def weigh(i):
            head = g * GROUP + i
            v = jnp.concatenate([v_tile[...], jnp.ones((width, HEAD_SIZE), BF16)], axis=1)
            added = jnp.dot(weight[i % held_heads, :, 0:width], v, preferred_element_type=F32)
            if is_first:
                sum_of[head] = added
                return
            rescale = top_of[1, head]
            held = sum_of[head]
            summed = held[:, :HEAD_SIZE] * rescale + added[:, :HEAD_SIZE]
            total = held[:, HEAD_SIZE:] * rescale + added[:, HEAD_SIZE:]
            if not is_last:
                sum_of[head, :, 0:HEAD_SIZE] = summed
                sum_of[head, :, HEAD_SIZE:] = total
                return
            attended = jnp.where(is_live, summed * (1.0 / total), 0.0)
            out[:, head_columns(head)] = attended.astype(BF16)
            total_all[...] = jnp.where(lane == head, total, total_all[...])

        if is_last:
            for step in range(GROUP + 1):
                if step < GROUP:
                    scores(step)
                if step >= 1:
                    soften(step - 1)
            await_values()
            for step in range(GROUP):
                weigh(step)
            return
        for step in range(GROUP + 2):
            if step < GROUP:
                scores(step)
            if 1 <= step <= GROUP:
                soften(step - 1)
            if step >= 2:
                weigh(step - 2)

    q_copy.wait()
    first[0].wait_recv()
    for copy in second:
        copy.start()

    @pl.loop(0, KEY_VALUE_HEADS)
    def _(g):
        absorb(g, own_k, own_v, ROWS, lambda: near_bias[...], True, False)

    def out_copy(g):
        wide = GROUP * HEAD_SIZE
        columns = pl.ds(pl.multiple_of(g * wide, wide), wide)
        return pltpu.make_async_copy(out.at[:, columns], out_ref.at[:, columns], out_sem.at[g])

    def pass_on(g):
        @pl.when((odd == 1) & (c >= 2))
        def _():
            for arriving, sending in zip(z_copies(g), onward_copies(g), strict=True):
                arriving.wait_recv()
                sending.start()

    pass_on(0)
    own_copy.wait()
    for copy in (*first[1:], *second):
        copy.wait_recv()
    third.start()
    pass_on(1)
    for copy in (*first, *second):
        copy.wait_send()
    third.wait()
    rows = prompt_raw[...].astype(F32)
    for g in range(KEY_VALUE_HEADS):
        lanes = slice(g * HEAD_SIZE, (g + 1) * HEAD_SIZE)
        other_k[0, g, ROWS:LAST] = rows[:, 0, lanes].astype(BF16)
        other_v[0, g, ROWS:LAST] = rows[:, 1, lanes].astype(BF16)

    @pl.loop(0, KEY_VALUE_HEADS)
    def _(g):
        @pl.when(odd == 0)
        def _():
            for arriving in z_copies(g):
                arriving.wait_recv()

        @pl.when(odd == 1)
        def _():
            for arriving in own_y_copies(g):
                arriving.wait_recv()

        absorb(g, other_k.at[0], other_v.at[0], LAST, lambda: early_bias, False, False)

        arriving_far = z_copies(g)
        passing = onward_copies(g)

        def await_part(part):
            @pl.when(odd == 0)
            def _():
                passing[part].wait_recv()

            @pl.when((odd == 1) & ((c < 2) | (g >= AHEAD)))
            def _():
                arriving_far[part].wait_recv()
                passing[part].start()

        def await_values():
            await_part(1)
            await_part(2)

        await_part(0)
        absorb(
            g, other_k.at[1], other_v.at[1], ROWS, lambda: late_bias, False, True, await_values
        )
        out_copy(g).start()

    log_total = ((top_all[...] + jnp.log2(total_all[...])) * LN2).T[:QUERY_HEADS]
    place = lax.broadcasted_iota(jnp.int32, (QUERY_HEADS, ROWS), 1)
    log_ref[...] = jnp.where(slot * ROWS + place < live_length, log_total, 0.0)

    for g in range(KEY_VALUE_HEADS):
        for copy in (*z_copies(g), *own_y_copies(g)):
            copy.wait_send()
        out_copy(g).wait()


def hand_on(attended_in, log_in, attended_out, log_out, held, held_log, in_sem, out_sem):
    pieces = 8
    rows = ROWS // pieces
    places = [pl.ds(i * rows, rows) for i in range(pieces)]
    inward = [pltpu.make_async_copy(attended_in.at[p], held.at[p], in_sem.at[i]) for i, p in enumerate(places)]
    outward = [pltpu.make_async_copy(held.at[p], attended_out.at[p], out_sem.at[i]) for i, p in enumerate(places)]
    inward.append(pltpu.make_async_copy(log_in, held_log, in_sem.at[pieces]))
    outward.append(pltpu.make_async_copy(held_log, log_out, out_sem.at[pieces]))
    for copy in inward:
        copy.start()
    for arriving, leaving in zip(inward, outward, strict=True):
        arriving.wait()
        leaving.start()
    for leaving in outward:
        leaving.wait()


def body(queries, resp_kv, prompt_kv, lengths, block_slot):
    hbm = pl.BlockSpec(memory_space=pltpu.HBM)
    smem = pl.BlockSpec(memory_space=pltpu.SMEM)
    vmem = pl.BlockSpec(memory_space=pltpu.VMEM)
    dma = pltpu.SemaphoreType.DMA
    block = pltpu.VMEM((KEY_VALUE_HEADS, ROWS, HEAD_SIZE), BF16)
    other = pltpu.VMEM((2, KEY_VALUE_HEADS, LAST, HEAD_SIZE), BF16)
    attended, log_total = pl.pallas_call(
        kernel,
        out_shape=(
            jax.ShapeDtypeStruct((ROWS, QUERY_HEADS * HEAD_SIZE), BF16),
            jax.ShapeDtypeStruct((QUERY_HEADS, ROWS), F32),
        ),
        in_specs=[hbm, hbm, hbm, smem, smem],
        out_specs=(hbm, vmem),
        scratch_shapes=[
            pltpu.VMEM((ROWS, QUERY_HEADS * HEAD_SIZE), BF16),
            pltpu.VMEM((KEY_VALUE_HEADS, ROWS, 2, HEAD_SIZE), BF16),
            pltpu.VMEM((PROMPT, 2, KEY_VALUE_HEADS * HEAD_SIZE), BF16),
            block, block, other, other,
            pltpu.VMEM((ROWS, ROWS), F32),
            pltpu.VMEM((2, QUERY_HEADS, ROWS, HEAD_SIZE), F32),
            pltpu.VMEM((QUERY_HEADS, ROWS, 2 * HEAD_SIZE), F32),
            pltpu.VMEM((ROWS, HEAD_SIZE), F32),
            pltpu.VMEM((ROWS, HEAD_SIZE), F32),
            pltpu.VMEM((2, ROWS, LAST), F32),
            pltpu.VMEM((GROUP, ROWS, LAST), BF16),
            pltpu.VMEM((ROWS, QUERY_HEADS * HEAD_SIZE), BF16),
            dma, dma((4,)), dma, dma((12,)), dma((12,)), dma((12,)), dma((12,)),
            dma((4,)), dma((4,)), dma((3,)), dma((3,)), dma, dma, dma((4,)),
        ],
        compiler_params=pltpu.CompilerParams(
            collective_id=0, has_side_effects=True, vmem_limit_bytes=63 * 1024 * 1024
        ),
    )(queries[0], resp_kv[0], prompt_kv[0], lengths, block_slot)
    attended, log_total = pl.pallas_call(
        hand_on,
        out_shape=(
            jax.ShapeDtypeStruct((ROWS, QUERY_HEADS * HEAD_SIZE), BF16),
            jax.ShapeDtypeStruct((QUERY_HEADS, ROWS), F32),
        ),
        in_specs=[hbm, hbm],
        out_specs=(hbm, hbm),
        scratch_shapes=[
            pltpu.VMEM((ROWS, QUERY_HEADS * HEAD_SIZE), BF16),
            pltpu.VMEM((QUERY_HEADS, ROWS), F32),
            dma((9,)), dma((9,)),
        ],
        compiler_params=pltpu.CompilerParams(vmem_limit_bytes=63 * 1024 * 1024),
    )(attended, log_total)
    return attended[None], log_total[None]


def solution(mesh):
    return jax.shard_map(
        body,
        mesh=mesh,
        in_specs=(
            P("resp", "ctx", None),
            P("resp", "ctx", None, None),
            P("ctx", "resp", None, None),
            P("resp"),
            P(),
        ),
        out_specs=(P("resp", "ctx", None), P("resp", None, "ctx")),
        check_vma=False,
    )
```
